32 devices in a mesh: dp: 8 (over y, x, core), tensor: 4 (over z).
Axes of the slice: x: 2, y: 2, z: 4, core: 2. Of those that a mesh axis runs over, the one named last changes fastest.
Arguments:
- tokens: bfloat16 [32, 8192], P('tensor', 'dp'), may hold values from -6 to 6
- out_grad: bfloat16 [32, 8192], P('tensor', 'dp'), may hold values from -6 to 6
- gate_weight: bfloat16 [8192, 15360], P('dp', 'tensor'), may hold values from -0.0625 to 0.0625
- up_weight: bfloat16 [8192, 15360], P('dp', 'tensor'), may hold values from -0.0625 to 0.0625
- down_weight: bfloat16 [15360, 8192], P('tensor', 'dp'), may hold values from -0.046875 to 0.046875
- gate_mask: int32 [64, 120], P('dp', 'tensor'), may hold values from 0 to 1
- up_mask: int32 [64, 120], P('dp', 'tensor'), may hold values from 0 to 1
- down_mask: int32 [120, 64], P('tensor', 'dp'), may hold values from 0 to 1
- counts: int32 [4], P('tensor'), may hold values from 1 to 8, 24 in all
Outputs:
- d_tokens: bfloat16 [32, 8192], P('tensor', 'dp')
- gate_sum: float32 [8192, 15360], P('dp', 'tensor')
- up_sum: float32 [8192, 15360], P('dp', 'tensor')
- down_sum: float32 [15360, 8192], P('tensor', 'dp')
The draws below stay inside these ranges and needn't reach their ends.
Inputs may be any that keep to these rules, and one draw needn't show every extreme that they name: counts[t] live rows open the t-th block of 8 token rows; at least one block is full.
All inputs are finite; a program needn't handle non-finite values.
Results may differ from the reference program's by a relative error of at most 0.005.
Values may be sent and summed in bfloat16 or wider, within the bound.
A program may use at most 128 MiB of HBM per device.

```python
import math
import jax
import jax.numpy as jnp
import numpy as np

D = 8192
FF = 15360
BLOCK = 128
TOK_DEV = 8
TOKENS = 32
N_TENSOR = 4


def draw_gate_mask(key, part):
    rates = jax.random.randint(jax.random.fold_in(key, 11), (1, FF // BLOCK), 2, 7)
    levels = jax.random.randint(jax.random.fold_in(key, 21), (D // BLOCK, FF // BLOCK), 0, 8)
    return (levels < rates).astype(jnp.int32)


def draw_up_mask(key, part):
    rates = jax.random.randint(jax.random.fold_in(key, 12), (1, FF // BLOCK), 2, 7)
    levels = jax.random.randint(jax.random.fold_in(key, 22), (D // BLOCK, FF // BLOCK), 0, 8)
    return (levels < rates).astype(jnp.int32)


def draw_down_mask(key, part):
    rates = jax.random.randint(jax.random.fold_in(key, 13), (FF // BLOCK, 1), 2, 7)
    levels = jax.random.randint(jax.random.fold_in(key, 23), (FF // BLOCK, D // BLOCK), 0, 8)
    return (levels < rates).astype(jnp.int32)


def level_of(rng, dims, shards, least, high):
    def one(axis_at, parts):
        draws = jax.random.uniform(jax.random.fold_in(jax.random.fold_in(rng, 6), axis_at), (parts,), jnp.float32, least / len(shards), high / len(shards))
        return jnp.repeat(jnp.exp(draws), dims[axis_at] // parts).reshape((-1,) + (1,) * (len(dims) - axis_at - 1))

    factor_of = one(*shards[0])
    for cut in shards[1:]:
        factor_of = factor_of * one(*cut)
    return factor_of


def split_up(count, total, limit, lean):
    loads = [(1 << 20) // math.isqrt(standing ** lean) + 1 for standing in range(2, count + 1)]
    rest, holding = total - limit - (count - 1), [1] * (count - 1)
    while rest > 0:
        movable = [i for i in range(count - 1) if holding[i] < limit]
        mass, budget = sum([loads[i] for i in movable]), rest
        for i in movable:
            addition = min(limit - holding[i], max(1, budget * loads[i] // mass), rest)
            holding[i] = holding[i] + addition
            rest = rest - addition
    return np.array([limit] + holding)


def ragged_sizes(key, number_of, total, reach, slope):
    if number_of == 2:
        one = jax.random.randint(key, (), max(1, total - reach), min(reach, total - 1) + 1)
        return jnp.stack([one, total - one])
    tallies = jnp.asarray(split_up(number_of, total, reach, slope), jnp.int32)
    pairs = (number_of - 1) // 2
    giver, sink = tallies[1:1 + 2 * pairs:2], tallies[2:2 + 2 * pairs:2]
    margin = jnp.minimum(giver - 1, reach - sink)
    shifted = jax.random.randint(jax.random.fold_in(key, 1), (pairs,), 0, 1 << 20) % (margin + 1)
    tallies = tallies.at[1:1 + 2 * pairs:2].set(giver - shifted).at[2:2 + 2 * pairs:2].set(sink + shifted)
    return tallies[jax.random.permutation(jax.random.fold_in(key, 2), number_of)]


def centred(own_key, shape, deviation, bound, shards=(), held_as=jnp.bfloat16):
    result = jax.random.normal(own_key, shape, jnp.float32) * deviation
    if len(shards) > 0:
        result = level_of(own_key, shape, shards, -0.22, 0.18) * result
    return jnp.clip(result, min=-bound, max=bound).astype(held_as)


def setup_inputs(seed: int = 0) -> dict:
    seeds = jax.random.split(jax.random.key(seed), 10)
    return {
        "tokens": centred(seeds[0], (TOKENS, D), 1.0, 6.0, ((0, 4), (1, 8))),
        "out_grad": centred(seeds[1], (TOKENS, D), 1.0, 6.0, ((0, 4), (1, 8))),
        "gate_weight": centred(seeds[2], (D, FF), D ** -0.5, 0.0625, ((0, 8), (1, 4))),
        "up_weight": centred(seeds[3], (D, FF), D ** -0.5, 0.0625, ((0, 8), (1, 4))),
        "down_weight": centred(seeds[4], (FF, D), FF ** -0.5, 0.046875, ((0, 4), (1, 8))),
        "gate_mask": draw_gate_mask(jax.random.fold_in(seeds[9], 71), 0),
        "up_mask": draw_up_mask(jax.random.fold_in(seeds[9], 71), 0),
        "down_mask": draw_down_mask(jax.random.fold_in(seeds[9], 71), 0),
        "counts": ragged_sizes(seeds[8], N_TENSOR, (3 * TOK_DEV * N_TENSOR) // 4, TOK_DEV, 2).astype(jnp.int32),
    }


def expand(mask):
    return jnp.repeat(jnp.repeat(mask, BLOCK, axis=0), BLOCK, axis=1)


def reference(tokens, out_grad, gate_weight, up_weight, down_weight, gate_mask, up_mask, down_mask, counts):
    row_index = jnp.arange(TOKENS, dtype=jnp.int32)
    is_valid = (row_index % TOK_DEV) < counts[row_index // TOK_DEV]
    masked_cot = jnp.where(is_valid[:, None], out_grad, jnp.zeros_like(out_grad))
    gate_keep = expand(gate_mask)
    up_keep = expand(up_mask)
    down_keep = expand(down_mask)
    masked_gate = gate_weight * gate_keep.astype(jnp.bfloat16)
    masked_up = up_weight * up_keep.astype(jnp.bfloat16)
    masked_down = down_weight * down_keep.astype(jnp.bfloat16)
    gate_pre = jnp.dot(tokens, masked_gate, preferred_element_type=jnp.float32)
    up_pre = jnp.dot(tokens, masked_up, preferred_element_type=jnp.float32)
    hidden_grad = jnp.dot(masked_cot, masked_down.T, preferred_element_type=jnp.float32)
    sigmoid_gate = jax.nn.sigmoid(gate_pre)
    activated = gate_pre * sigmoid_gate
    hidden = (activated * up_pre).astype(jnp.bfloat16)
    gate_grad = (hidden_grad * up_pre * sigmoid_gate * (1.0 + gate_pre * (1.0 - sigmoid_gate))).astype(jnp.bfloat16)
    up_grad = (hidden_grad * activated).astype(jnp.bfloat16)
    d_tokens = jnp.dot(gate_grad, masked_gate.T, preferred_element_type=jnp.float32)
    d_tokens = d_tokens + jnp.dot(up_grad, masked_up.T, preferred_element_type=jnp.float32)
    gate_sum = jnp.dot(tokens.T, gate_grad, preferred_element_type=jnp.float32) * gate_keep.astype(jnp.float32)
    up_sum = jnp.dot(tokens.T, up_grad, preferred_element_type=jnp.float32) * up_keep.astype(jnp.float32)
    down_sum = jnp.dot(hidden.T, masked_cot, preferred_element_type=jnp.float32) * down_keep.astype(jnp.float32)
    return (d_tokens.astype(jnp.bfloat16), gate_sum, up_sum, down_sum)
```

```python
import functools

import jax
import jax.numpy as jnp
from jax import lax
from jax.experimental import pallas as pl
from jax.experimental.pallas import tpu as pltpu
from jax.sharding import PartitionSpec as P

MESH = pl.DeviceIdType.MESH
LANES = 128
bf16, f32 = jnp.bfloat16, jnp.float32


def dot_nn(a, b):
    return jnp.dot(a, b, preferred_element_type=f32)


def dot_nt(a, b):
    return lax.dot_general(a, b, (((1,), (1,)), ((), ())), preferred_element_type=f32)


def splat(value):
    return jnp.full((16, LANES), value.astype(f32), f32).astype(bf16)


def masked_tile(block, keeps):
    keep = jnp.concatenate([splat(k) for k in keeps], axis=1) if len(keeps) > 1 else splat(keeps[0])
    rows, cols = block.shape
    return (block.reshape(rows // 16, 16, cols) * keep[None]).reshape(rows, cols)


def swiglu_parts(gate_pre, up_pre, hidden_grad):
    sig = jax.nn.sigmoid(gate_pre)
    activated = gate_pre * sig
    hidden = (activated * up_pre).astype(bf16)
    gate_grad = (hidden_grad * up_pre * sig * (1.0 + gate_pre * (1.0 - sig))).astype(bf16)
    up_grad = (hidden_grad * activated).astype(bf16)
    return gate_grad, up_grad, hidden


def exchange_kernel(
    ndp, nt, nq, pw, nchunk,
    tok_ref, cot_ref, gate_hbm, up_hbm, down_hbm, gmask, umask, dmask, counts,
    dtok_ref, act_ref, tokall_ref, cotall_ref,
    gw, uw, dw, xs, snd1, own1, rcv1, snd2, rcv2, acts, dacc, dsnd, drcv,
    wsem, xs_s, xs_r, s1_s, s1_r, s2_s, s2_r, ag_s, ag_r, fw_s, fw_r, dt_s, dt_r,
):
    nchip = ndp // 2
    tr, width = tok_ref.shape
    kblocks = width // LANES
    me = lax.axis_index("dp")
    mt = lax.axis_index("tensor")
    core = lax.rem(me, 2)
    chip = me // 2
    sibling = chip * 2 + (1 - core)

    def weight_copies(q):
        cols = pl.ds(pl.multiple_of(q * pw, pw), pw)
        return (
            pltpu.make_async_copy(gate_hbm.at[:, cols], gw.at[q], wsem.at[q, 0]),
            pltpu.make_async_copy(up_hbm.at[:, cols], uw.at[q], wsem.at[q, 1]),
            pltpu.make_async_copy(down_hbm.at[cols, :], dw.at[q], wsem.at[q, 2]),
        )

    def each_piece(c, k, last):
        return c * ndp + 2 * k + (core if last else 1 - core)

    for c in range(nchunk):
        def load(k, _, c=c):
            for last in (False, True):
                q = each_piece(c, k, last)

                @pl.when(q < nq)
                def _():
                    for copy in weight_copies(q):
                        copy.start()
            return 0
        lax.fori_loop(0, nchip, load, 0)

    live = lax.broadcasted_iota(jnp.int32, (tr, width), 0) < counts[0]
    cot = jnp.where(live, cot_ref[...].astype(f32), 0.0)
    xs[mt] = jnp.concatenate([tok_ref[...].astype(f32), cot], axis=0).astype(bf16)

    barrier = pltpu.get_barrier_semaphore()
    pl.semaphore_signal(barrier, inc=1, device_id=(sibling, mt), device_id_type=MESH)

    def greet_chip(j, _):
        peer = lax.rem(chip + j, nchip) * 2 + core
        pl.semaphore_signal(barrier, inc=1, device_id=(peer, mt), device_id_type=MESH)
        return 0

    def greet_tensor(j, _):
        pl.semaphore_signal(barrier, inc=1, device_id=(me, lax.rem(mt + j, nt)), device_id_type=MESH)
        return 0

    lax.fori_loop(1, nchip, greet_chip, 0)
    lax.fori_loop(1, nt, greet_tensor, 0)
    pl.semaphore_wait(barrier, 1 + (nchip - 1) + (nt - 1))

    def x_copy(slot, j, peer):
        return pltpu.make_async_remote_copy(
            src_ref=xs.at[slot], dst_ref=xs.at[slot], send_sem=xs_s.at[j],
            recv_sem=xs_r.at[slot], device_id=(me, peer), device_id_type=MESH)

    def x_send(j, _):
        x_copy(mt, j, lax.rem(mt + j, nt)).start()
        return 0

    def x_wait(j, _):
        peer = lax.rem(mt + j, nt)
        x_copy(peer, j, peer).wait_recv()
        return 0

    def x_sent(j, _):
        x_copy(mt, j, lax.rem(mt + j, nt)).wait_send()
        return 0

    lax.fori_loop(1, nt, x_send, 0)
    lax.fori_loop(1, nt, x_wait, 0)
    gathered = xs[...].astype(f32)
    tokall_ref[...] = gathered[:, :tr].reshape(nt * tr, width).astype(bf16)
    cotall_ref[...] = gathered[:, tr:].reshape(nt * tr, width).astype(bf16)
    rows = nt * tr

    def forward_piece(q, out):
        @pl.when(q < nq)
        def _():
            for copy in weight_copies(q):
                copy.wait()
            per = pw // LANES
            for w, mask, slot in ((gw, gmask, 0), (uw, umask, 1)):
                for kb in range(kblocks):
                    span = pl.ds(kb * LANES, LANES)
                    w[q, span, :] = masked_tile(w[q, span, :], [mask[kb, q * per + i] for i in range(per)])
                out[slot] = dot_nn(tokall_ref[...], w[q])
            for i in range(per):
                span = pl.ds(i * LANES, LANES)
                dw[q, span, :] = masked_tile(dw[q, span, :], [dmask[q * per + i, kb] for kb in range(kblocks)])
            out[2] = dot_nt(cotall_ref[...], dw[q])

        @pl.when(q >= nq)
        def _():
            out[...] = jnp.zeros(out.shape, out.dtype)

    def copy1(c, k):
        return pltpu.make_async_remote_copy(
            src_ref=snd1.at[c, k], dst_ref=rcv1.at[c, k], send_sem=s1_s.at[c, k],
            recv_sem=s1_r.at[c, k], device_id=(sibling, mt), device_id_type=MESH)

    def forward(c):
        def step(k, _):
            forward_piece(each_piece(c, k, False), snd1.at[c, k])
            copy1(c, k).start()
            forward_piece(each_piece(c, k, True), own1.at[c, k])
            return 0
        lax.fori_loop(0, nchip, step, 0)

    def copy2(c, slot, k):
        return pltpu.make_async_remote_copy(
            src_ref=snd2.at[c, k], dst_ref=rcv2.at[c, slot], send_sem=s2_s.at[c, k],
            recv_sem=s2_r.at[c, slot], device_id=(k * 2 + core, mt), device_id_type=MESH)

    def reduce_send(c):
        def step(j, _):
            k = lax.rem(chip + j, nchip)
            copy1(c, k).wait_recv()
            snd2[c, k] = (own1[c, k] + rcv1[c, k]).astype(bf16)
            copy2(c, chip, k).start()
            return 0
        lax.fori_loop(1, nchip, step, 0)
        copy1(c, chip).wait_recv()

    def gather_copy(c, origin, sem, k):
        slot = c * ndp + origin
        return pltpu.make_async_remote_copy(
            src_ref=acts.at[slot], dst_ref=acts.at[slot], send_sem=ag_s.at[c, sem],
            recv_sem=ag_r.at[c, origin // 2], device_id=(k * 2 + core, mt), device_id_type=MESH)

    def sibling_copy(c, origin):
        slot = c * ndp + origin
        return pltpu.make_async_remote_copy(
            src_ref=acts.at[slot], dst_ref=acts.at[slot], send_sem=fw_s.at[c, origin // 2],
            recv_sem=fw_r.at[c, origin // 2], device_id=(sibling, mt), device_id_type=MESH)

    def activate(c):
        own1[c, chip] = own1[c, chip] + rcv1[c, chip]

        def add(j, _):
            k = lax.rem(chip + j, nchip)
            copy2(c, k, k).wait_recv()
            own1[c, chip] = own1[c, chip] + rcv2[c, k].astype(f32)
            return 0
        lax.fori_loop(1, nchip, add, 0)
        parts = swiglu_parts(own1[c, chip, 0], own1[c, chip, 1], own1[c, chip, 2])
        for i in range(3):
            acts[c * ndp + me, i] = parts[i]

        def send(j, _):
            gather_copy(c, me, j, lax.rem(chip + j, nchip)).start()
            return 0
        lax.fori_loop(1, nchip, send, 0)
        sibling_copy(c, me).start()

    def forward_on(c):
        def step(j, _):
            k = lax.rem(chip + j, nchip)
            gather_copy(c, k * 2 + core, j, k).wait_recv()
            sibling_copy(c, k * 2 + core).start()
            return 0
        lax.fori_loop(1, nchip, step, 0)

        def wait(k, _):
            sibling_copy(c, k * 2 + 1 - core).wait_recv()
            return 0
        lax.fori_loop(0, nchip, wait, 0)

    def token_grad(lo, hi):
        def step(q, _):
            dacc[...] += dot_nt(acts[q, 0], gw[q]) + dot_nt(acts[q, 1], uw[q])
            return 0
        if hi > lo:
            lax.fori_loop(lo, hi, step, 0)

    dacc[...] = jnp.zeros(dacc.shape, f32)
    for c in range(nchunk):
        forward(c)
        if c > 0:
            activate(c - 1)
        reduce_send(c)
        if c > 0:
            forward_on(c - 1)
    done = min((nchunk - 1) * ndp, nq)
    token_grad(0, done // 2)
    activate(nchunk - 1)
    token_grad(done // 2, done)
    forward_on(nchunk - 1)
    token_grad(done, nq)

    dsnd[...] = dacc[...].reshape(nt, tr, width)

    def d_copy(slot, k):
        return pltpu.make_async_remote_copy(
            src_ref=dsnd.at[k], dst_ref=drcv.at[slot], send_sem=dt_s.at[k],
            recv_sem=dt_r.at[slot], device_id=(me, k), device_id_type=MESH)

    def d_send(j, _):
        k = lax.rem(mt + nt - j, nt)
        d_copy(mt, k).start()
        return 0

    lax.fori_loop(1, nt, d_send, 0)
    act_ref[...] = acts[...]
    lax.fori_loop(1, nt, x_sent, 0)
    for c in range(nchunk):
        def drain(k, _, c=c):
            copy1(c, k).wait_send()
            sibling_copy(c, k * 2 + core).wait_send()
            return 0

        def drain_chips(j, _, c=c):
            k = lax.rem(chip + j, nchip)
            copy2(c, chip, k).wait_send()
            gather_copy(c, me, j, k).wait_send()
            return 0
        lax.fori_loop(0, nchip, drain, 0)
        lax.fori_loop(1, nchip, drain_chips, 0)

    def d_add(j, total):
        k = lax.rem(mt + j, nt)
        d_copy(k, k).wait_recv()
        return total + drcv[k]

    dtok_ref[...] = lax.fori_loop(1, nt, d_add, dsnd[mt]).astype(bf16)

    def d_sent(j, _):
        d_copy(mt, lax.rem(mt + j, nt)).wait_send()
        return 0
    lax.fori_loop(1, nt, d_sent, 0)


def outer_kernel(
    pw, gmask, umask, dmask, tok_ref, cot_ref, act_ref, gsum_ref, usum_ref, dsum_ref, tok_t
):
    q = pl.program_id(0)
    width = tok_ref.shape[1]
    per = pw // LANES

    @pl.when(q == 0)
    def _():
        tok_t[...] = tok_ref[...].astype(f32).T.astype(bf16)

    for slot, mask, out in ((0, gmask, gsum_ref), (1, umask, usum_ref)):
        for kb in range(width // LANES):
            span = pl.ds(kb * LANES, LANES)
            block = dot_nn(tok_t[span, :], act_ref[0, slot])
            for i in range(per):
                cols = slice(i * LANES, (i + 1) * LANES)
                out[span, cols] = block[:, cols] * mask[kb, q * per + i].astype(f32)
    hidden_t = act_ref[0, 2].astype(f32).T.astype(bf16)
    for i in range(per):
        block = dot_nn(hidden_t[i * LANES:(i + 1) * LANES], cot_ref[...])
        for kb in range(width // LANES):
            cols = slice(kb * LANES, (kb + 1) * LANES)
            dsum_ref[pl.ds(i * LANES, LANES), cols] = block[:, cols] * dmask[q * per + i, kb].astype(f32)


def on_device(
    ndp, nt, tokens, out_grad, gate_weight, up_weight, down_weight, gate_mask, up_mask, down_mask, counts
):
    tr, width = tokens.shape
    hidden_width = gate_weight.shape[1]
    rows = nt * tr
    pw = 2 * LANES if hidden_width % (2 * LANES) == 0 else LANES
    nq = hidden_width // pw
    nchunk = -(-nq // ndp)
    nchip = ndp // 2
    vmem = pl.BlockSpec(memory_space=pltpu.VMEM)
    smem = pl.BlockSpec(memory_space=pltpu.SMEM)
    hbm = pl.BlockSpec(memory_space=pl.ANY)
    dma = pltpu.SemaphoreType.DMA
    piece = (3, rows, pw)
    d_tokens, act, tok_all, cot_all = pl.pallas_call(
        functools.partial(exchange_kernel, ndp, nt, nq, pw, nchunk),
        out_shape=(
            jax.ShapeDtypeStruct((tr, width), bf16),
            jax.ShapeDtypeStruct((nchunk * ndp,) + piece, bf16),
            jax.ShapeDtypeStruct((rows, width), bf16),
            jax.ShapeDtypeStruct((rows, width), bf16),
        ),
        in_specs=[vmem, vmem, hbm, hbm, hbm, smem, smem, smem, smem],
        out_specs=(vmem, vmem, vmem, vmem),
        scratch_shapes=[
            pltpu.VMEM((nq, width, pw), bf16),
            pltpu.VMEM((nq, width, pw), bf16),
            pltpu.VMEM((nq, pw, width), bf16),
            pltpu.VMEM((nt, 2 * tr, width), bf16),
            pltpu.VMEM((nchunk, nchip) + piece, f32),
            pltpu.VMEM((nchunk, nchip) + piece, f32),
            pltpu.VMEM((nchunk, nchip) + piece, f32),
            pltpu.VMEM((nchunk, nchip) + piece, bf16),
            pltpu.VMEM((nchunk, nchip) + piece, bf16),
            pltpu.VMEM((nchunk * ndp,) + piece, bf16),
            pltpu.VMEM((rows, width), f32),
            pltpu.VMEM((nt, tr, width), f32),
            pltpu.VMEM((nt, tr, width), f32),
            dma((nq, 3)),
            dma((nt,)), dma((nt,)),
            dma((nchunk, nchip)), dma((nchunk, nchip)),
            dma((nchunk, nchip)), dma((nchunk, nchip)),
            dma((nchunk, nchip)), dma((nchunk, nchip)),
            dma((nchunk, nchip)), dma((nchunk, nchip)),
            dma((nt,)), dma((nt,)),
        ],
        compiler_params=pltpu.CompilerParams(
            collective_id=0, has_side_effects=True, vmem_limit_bytes=58 * 2**20
        ),
        name="exchange",
    )(tokens, out_grad, gate_weight, up_weight, down_weight, gate_mask, up_mask, down_mask, counts)

    whole = lambda q, *_: (0, 0)
    gate_sum, up_sum, down_sum = pl.pallas_call(
        functools.partial(outer_kernel, pw),
        grid_spec=pltpu.PrefetchScalarGridSpec(
            num_scalar_prefetch=3,
            grid=(nq,),
            in_specs=[
                pl.BlockSpec((rows, width), whole),
                pl.BlockSpec((rows, width), whole),
                pl.BlockSpec((1,) + piece, lambda q, *_: (q, 0, 0, 0)),
            ],
            out_specs=[
                pl.BlockSpec((width, pw), lambda q, *_: (0, q)),
                pl.BlockSpec((width, pw), lambda q, *_: (0, q)),
                pl.BlockSpec((pw, width), lambda q, *_: (q, 0)),
            ],
            scratch_shapes=[pltpu.VMEM((width, rows), bf16)],
        ),
        out_shape=(
            jax.ShapeDtypeStruct((width, hidden_width), f32),
            jax.ShapeDtypeStruct((width, hidden_width), f32),
            jax.ShapeDtypeStruct((hidden_width, width), f32),
        ),
        compiler_params=pltpu.CompilerParams(vmem_limit_bytes=40 * 2**20),
        name="outer",
    )(gate_mask, up_mask, down_mask, tok_all, cot_all, act)
    return d_tokens, gate_sum, up_sum, down_sum


def solution(mesh):
    in_specs = (
        P("tensor", "dp"),
        P("tensor", "dp"),
        P("dp", "tensor"),
        P("dp", "tensor"),
        P("tensor", "dp"),
        P("dp", "tensor"),
        P("dp", "tensor"),
        P("tensor", "dp"),
        P("tensor"),
    )
    out_specs = (P("tensor", "dp"), P("dp", "tensor"), P("dp", "tensor"), P("tensor", "dp"))
    body = functools.partial(on_device, mesh.shape["dp"], mesh.shape["tensor"])
    return jax.shard_map(body, mesh=mesh, in_specs=in_specs, out_specs=out_specs, check_vma=False)
```

```python
import functools

import jax
import jax.numpy as jnp
from jax import lax
from jax.experimental import pallas as pl
from jax.experimental.pallas import tpu as pltpu
from jax.sharding import PartitionSpec as P

MESH = pl.DeviceIdType.MESH
LANES = 128
bf16, f32 = jnp.bfloat16, jnp.float32


def dot_nn(a, b):
    return jnp.dot(a, b, preferred_element_type=f32)


def dot_nt(a, b):
    return lax.dot_general(a, b, (((1,), (1,)), ((), ())), preferred_element_type=f32)


def keep_tile(keeps):
    tiles = [jnp.full((16, LANES), k.astype(f32), f32).astype(bf16) for k in keeps]
    return jnp.concatenate(tiles, axis=1) if len(tiles) > 1 else tiles[0]


def masked(rows, keeps):
    count, cols = rows.shape
    return (rows.reshape(count // 16, 16, cols) * keep_tile(keeps)[None]).reshape(count, cols)


def masked_stack(rows, keep_lists):
    copies = [masked(rows, keeps) for keeps in keep_lists]
    return jnp.concatenate(copies, axis=0) if len(copies) > 1 else copies[0]


def swiglu_parts(gate_pre, up_pre, hidden_grad):
    sig = jax.nn.sigmoid(gate_pre)
    activated = gate_pre * sig
    hidden = (activated * up_pre).astype(bf16)
    gate_grad = (hidden_grad * up_pre * sig * (1.0 + gate_pre * (1.0 - sig))).astype(bf16)
    up_grad = (hidden_grad * activated).astype(bf16)
    return gate_grad, up_grad, hidden


def exchange_kernel(
    ndp, nt, nq, pw, nchunk,
    tok_ref, cot_ref, gate_hbm, up_hbm, down_hbm, gmask, umask, dmask, counts,
    dtok_ref, act_ref, x_ref,
    gw, uw, dw, xs, tokall, cotall, snd1, own1, rcv1, snd2, rcv2, acts, dacc, dsnd, drcv,
    wsem, out_sem, xs_s, xs_r, s1_s, s1_r, s2_s, s2_r, ag_s, ag_r, fw_s, fw_r, dt_s, dt_r,
):
    nchip = ndp // 2
    tr, width = tok_ref.shape
    kblocks = width // LANES
    me = lax.axis_index("dp")
    mt = lax.axis_index("tensor")
    core = lax.rem(me, 2)
    chip = me // 2
    sibling = chip * 2 + (1 - core)

    def weight_copies(q):
        cols = pl.ds(pl.multiple_of(q * pw, pw), pw)
        return (
            pltpu.make_async_copy(gate_hbm.at[:, cols], gw.at[q], wsem.at[q, 0]),
            pltpu.make_async_copy(up_hbm.at[:, cols], uw.at[q], wsem.at[q, 1]),
            pltpu.make_async_copy(down_hbm.at[cols, :], dw.at[q], wsem.at[q, 2]),
        )

    def each_piece(c, k, last):
        return c * ndp + 2 * k + (core if last else 1 - core)

    for c in range(nchunk):
        def load(k, _, c=c):
            for last in (False, True):
                q = each_piece(c, k, last)

                @pl.when(q < nq)
                def _():
                    for copy in weight_copies(q):
                        copy.start()
            return 0
        lax.fori_loop(0, nchip, load, 0)

    live = lax.broadcasted_iota(jnp.int32, (tr, width), 0) < counts[0]
    cot = jnp.where(live, cot_ref[...].astype(f32), 0.0)
    xs[mt] = jnp.concatenate([tok_ref[...].astype(f32), cot], axis=0).astype(bf16)

    barrier = pltpu.get_barrier_semaphore()
    pl.semaphore_signal(barrier, inc=1, device_id=(sibling, mt), device_id_type=MESH)

    def greet_chip(j, _):
        peer = lax.rem(chip + j, nchip) * 2 + core
        pl.semaphore_signal(barrier, inc=1, device_id=(peer, mt), device_id_type=MESH)
        return 0

    def greet_tensor(j, _):
        pl.semaphore_signal(barrier, inc=1, device_id=(me, lax.rem(mt + j, nt)), device_id_type=MESH)
        return 0

    lax.fori_loop(1, nchip, greet_chip, 0)
    lax.fori_loop(1, nt, greet_tensor, 0)
    pl.semaphore_wait(barrier, 1 + (nchip - 1) + (nt - 1))

    def x_copy(slot, j, peer):
        return pltpu.make_async_remote_copy(
            src_ref=xs.at[slot], dst_ref=xs.at[slot], send_sem=xs_s.at[j],
            recv_sem=xs_r.at[slot], device_id=(me, peer), device_id_type=MESH)

    def x_send(j, _):
        x_copy(mt, j, lax.rem(mt + j, nt)).start()
        return 0

    def x_wait(j, _):
        peer = lax.rem(mt + j, nt)
        x_copy(peer, j, peer).wait_recv()
        return 0

    def x_sent(j, _):
        x_copy(mt, j, lax.rem(mt + j, nt)).wait_send()
        return 0

    lax.fori_loop(1, nt, x_send, 0)
    lax.fori_loop(1, nt, x_wait, 0)
    gathered = xs[...].astype(f32)
    tokall[...] = gathered[:, :tr].reshape(nt * tr, width).astype(bf16)
    cotall[...] = gathered[:, tr:].reshape(nt * tr, width).astype(bf16)
    x_out = pltpu.make_async_copy(xs, x_ref, out_sem.at[nchunk])
    x_out.start()
    rows = nt * tr
    per = pw // LANES
    pair = 2 if kblocks % 2 == 0 else 1

    def forward_piece(q, out):
        @pl.when(q < nq)
        def _():
            for copy in weight_copies(q):
                copy.wait()
            for w, mask, slot in ((gw, gmask, 0), (uw, umask, 1), (dw, dmask, 2)):
                source = cotall if slot == 2 else tokall
                left = masked_stack(
                    source[...],
                    [[mask[kb, q * per + i] for kb in range(kblocks)] for i in range(per)])
                sums = dot_nt(left, w[q]) if slot == 2 else dot_nn(left, w[q])
                for i in range(per):
                    cols = slice(i * LANES, (i + 1) * LANES)
                    out[slot, :, cols] = sums[i * rows:(i + 1) * rows, cols]

        @pl.when(q >= nq)
        def _():
            out[...] = jnp.zeros(out.shape, out.dtype)

    def copy1(c, k):
        return pltpu.make_async_remote_copy(
            src_ref=snd1.at[c, k], dst_ref=rcv1.at[c, k], send_sem=s1_s.at[c, k],
            recv_sem=s1_r.at[c, k], device_id=(sibling, mt), device_id_type=MESH)

    def forward(c):
        def step(k, _):
            forward_piece(each_piece(c, k, False), snd1.at[c, k])
            copy1(c, k).start()
            forward_piece(each_piece(c, k, True), own1.at[c, k])
            return 0
        lax.fori_loop(0, nchip, step, 0)

    def copy2(c, slot, k):
        return pltpu.make_async_remote_copy(
            src_ref=snd2.at[c, k], dst_ref=rcv2.at[c, slot], send_sem=s2_s.at[c, k],
            recv_sem=s2_r.at[c, slot], device_id=(k * 2 + core, mt), device_id_type=MESH)

    def reduce_send(c):
        def step(j, _):
            k = lax.rem(chip + j, nchip)
            copy1(c, k).wait_recv()
            snd2[c, k] = (own1[c, k] + rcv1[c, k]).astype(bf16)
            copy2(c, chip, k).start()
            return 0
        lax.fori_loop(1, nchip, step, 0)
        copy1(c, chip).wait_recv()

    def gather_copy(c, origin, sem, k):
        slot = c * ndp + origin
        return pltpu.make_async_remote_copy(
            src_ref=acts.at[slot], dst_ref=acts.at[slot], send_sem=ag_s.at[c, sem],
            recv_sem=ag_r.at[c, origin // 2], device_id=(k * 2 + core, mt), device_id_type=MESH)

    def sibling_copy(c, origin):
        slot = c * ndp + origin
        return pltpu.make_async_remote_copy(
            src_ref=acts.at[slot], dst_ref=acts.at[slot], send_sem=fw_s.at[c, origin // 2],
            recv_sem=fw_r.at[c, origin // 2], device_id=(sibling, mt), device_id_type=MESH)

    def activate(c):
        own1[c, chip] = own1[c, chip] + rcv1[c, chip]

        def add(j, _):
            k = lax.rem(chip + j, nchip)
            copy2(c, k, k).wait_recv()
            own1[c, chip] = own1[c, chip] + rcv2[c, k].astype(f32)
            return 0
        lax.fori_loop(1, nchip, add, 0)
        parts = swiglu_parts(own1[c, chip, 0], own1[c, chip, 1], own1[c, chip, 2])
        for i in range(3):
            acts[c * ndp + me, i] = parts[i]

        def send(j, _):
            gather_copy(c, me, j, lax.rem(chip + j, nchip)).start()
            return 0
        lax.fori_loop(1, nchip, send, 0)
        sibling_copy(c, me).start()

    def forward_on(c):
        def step(j, _):
            k = lax.rem(chip + j, nchip)
            gather_copy(c, k * 2 + core, j, k).wait_recv()
            sibling_copy(c, k * 2 + core).start()
            return 0
        lax.fori_loop(1, nchip, step, 0)

        def wait(k, _):
            sibling_copy(c, k * 2 + 1 - core).wait_recv()
            return 0
        lax.fori_loop(0, nchip, wait, 0)

    def token_grad(lo, hi):
        def step(q, _):
            for first in range(0, kblocks, pair):
                blocks = range(first, first + pair)
                span = pl.ds(first * LANES, pair * LANES)
                sums = None
                for w, mask, slot in ((gw, gmask, 0), (uw, umask, 1)):
                    left = masked_stack(
                        acts[q, slot], [[mask[kb, q * per + i] for i in range(per)] for kb in blocks])
                    term = dot_nt(left, w[q, span, :])
                    sums = term if sums is None else sums + term
                for i, kb in enumerate(blocks):
                    cols = slice(i * LANES, (i + 1) * LANES)
                    dacc[:, kb * LANES:(kb + 1) * LANES] += sums[i * rows:(i + 1) * rows, cols]
            return 0
        if hi > lo:
            lax.fori_loop(lo, hi, step, 0)

    def act_out(c):
        span = pl.ds(c * ndp, ndp)
        return pltpu.make_async_copy(acts.at[span], act_ref.at[span], out_sem.at[c])

    dacc[...] = jnp.zeros(dacc.shape, f32)
    for c in range(nchunk):
        forward(c)
        if c > 0:
            activate(c - 1)
        reduce_send(c)
        if c > 0:
            forward_on(c - 1)
            act_out(c - 1).start()
    done = min((nchunk - 1) * ndp, nq)
    token_grad(0, done // 2)
    activate(nchunk - 1)
    token_grad(done // 2, done)
    forward_on(nchunk - 1)
    act_out(nchunk - 1).start()
    token_grad(done, nq)

    dsnd[...] = dacc[...].reshape(nt, tr, width)

    def d_copy(slot, k):
        return pltpu.make_async_remote_copy(
            src_ref=dsnd.at[k], dst_ref=drcv.at[slot], send_sem=dt_s.at[k],
            recv_sem=dt_r.at[slot], device_id=(me, k), device_id_type=MESH)

    def d_send(j, _):
        k = lax.rem(mt + nt - j, nt)
        d_copy(mt, k).start()
        return 0

    lax.fori_loop(1, nt, d_send, 0)
    lax.fori_loop(1, nt, x_sent, 0)
    for c in range(nchunk):
        def drain(k, _, c=c):
            copy1(c, k).wait_send()
            sibling_copy(c, k * 2 + core).wait_send()
            return 0

        def drain_chips(j, _, c=c):
            k = lax.rem(chip + j, nchip)
            copy2(c, chip, k).wait_send()
            gather_copy(c, me, j, k).wait_send()
            return 0
        lax.fori_loop(0, nchip, drain, 0)
        lax.fori_loop(1, nchip, drain_chips, 0)

    def d_add(j, total):
        k = lax.rem(mt + j, nt)
        d_copy(k, k).wait_recv()
        return total + drcv[k]

    dtok_ref[...] = lax.fori_loop(1, nt, d_add, dsnd[mt]).astype(bf16)

    def d_sent(j, _):
        d_copy(mt, lax.rem(mt + j, nt)).wait_send()
        return 0
    lax.fori_loop(1, nt, d_sent, 0)
    x_out.wait()
    for c in range(nchunk):
        act_out(c).wait()


def outer_kernel(
    pw, gmask, umask, dmask, x_ref, act_ref, dtok_ref, dtok_out, gsum_ref, usum_ref, dsum_ref, tok_t, cot
):
    q = pl.program_id(0)
    nt, pair_rows, width = x_ref.shape
    tr = pair_rows // 2
    per = pw // LANES

    @pl.when(q == 0)
    def _():
        gathered = x_ref[...].astype(f32)
        tok_t[...] = gathered[:, :tr].reshape(nt * tr, width).T.astype(bf16)
        cot[...] = gathered[:, tr:].reshape(nt * tr, width).astype(bf16)
        dtok_out[...] = dtok_ref[...]

    for slot, mask, out in ((0, gmask, gsum_ref), (1, umask, usum_ref)):
        for kb in range(width // LANES):
            span = pl.ds(kb * LANES, LANES)
            block = dot_nn(tok_t[span, :], act_ref[0, slot])
            for i in range(per):
                cols = slice(i * LANES, (i + 1) * LANES)
                out[span, cols] = block[:, cols] * mask[kb, q * per + i].astype(f32)
    hidden_t = act_ref[0, 2].astype(f32).T.astype(bf16)
    for i in range(per):
        block = dot_nn(hidden_t[i * LANES:(i + 1) * LANES], cot[...])
        for kb in range(width // LANES):
            cols = slice(kb * LANES, (kb + 1) * LANES)
            dsum_ref[pl.ds(i * LANES, LANES), cols] = block[:, cols] * dmask[kb, q * per + i].astype(f32)


def on_device(
    ndp, nt, tokens, out_grad, gate_weight, up_weight, down_weight, gate_mask, up_mask, down_mask, counts
):
    tr, width = tokens.shape
    hidden_width = gate_weight.shape[1]
    rows = nt * tr
    pw = 2 * LANES if hidden_width % (2 * LANES) == 0 else LANES
    nq = hidden_width // pw
    nchunk = -(-nq // ndp)
    nchip = ndp // 2
    vmem = pl.BlockSpec(memory_space=pltpu.VMEM)
    smem = pl.BlockSpec(memory_space=pltpu.SMEM)
    hbm = pl.BlockSpec(memory_space=pl.ANY)
    dma = pltpu.SemaphoreType.DMA
    piece = (3, rows, pw)
    down_mask = down_mask.T
    d_tokens, act, gathered = pl.pallas_call(
        functools.partial(exchange_kernel, ndp, nt, nq, pw, nchunk),
        out_shape=(
            jax.ShapeDtypeStruct((tr, width), bf16),
            jax.ShapeDtypeStruct((nchunk * ndp,) + piece, bf16),
            jax.ShapeDtypeStruct((nt, 2 * tr, width), bf16),
        ),
        in_specs=[vmem, vmem, hbm, hbm, hbm, smem, smem, smem, smem],
        out_specs=(vmem, hbm, hbm),
        scratch_shapes=[
            pltpu.VMEM((nq, width, pw), bf16),
            pltpu.VMEM((nq, width, pw), bf16),
            pltpu.VMEM((nq, pw, width), bf16),
            pltpu.VMEM((nt, 2 * tr, width), bf16),
            pltpu.VMEM((rows, width), bf16),
            pltpu.VMEM((rows, width), bf16),
            pltpu.VMEM((nchunk, nchip) + piece, f32),
            pltpu.VMEM((nchunk, nchip) + piece, f32),
            pltpu.VMEM((nchunk, nchip) + piece, f32),
            pltpu.VMEM((nchunk, nchip) + piece, bf16),
            pltpu.VMEM((nchunk, nchip) + piece, bf16),
            pltpu.VMEM((nchunk * ndp,) + piece, bf16),
            pltpu.VMEM((rows, width), f32),
            pltpu.VMEM((nt, tr, width), f32),
            pltpu.VMEM((nt, tr, width), f32),
            dma((nq, 3)), dma((nchunk + 1,)),
            dma((nt,)), dma((nt,)),
            dma((nchunk, nchip)), dma((nchunk, nchip)),
            dma((nchunk, nchip)), dma((nchunk, nchip)),
            dma((nchunk, nchip)), dma((nchunk, nchip)),
            dma((nchunk, nchip)), dma((nchunk, nchip)),
            dma((nt,)), dma((nt,)),
        ],
        compiler_params=pltpu.CompilerParams(
            collective_id=0, has_side_effects=True, vmem_limit_bytes=58 * 2**20
        ),
        name="exchange",
    )(tokens, out_grad, gate_weight, up_weight, down_weight, gate_mask, up_mask, down_mask, counts)

    d_tokens, gate_sum, up_sum, down_sum = pl.pallas_call(
        functools.partial(outer_kernel, pw),
        grid_spec=pltpu.PrefetchScalarGridSpec(
            num_scalar_prefetch=3,
            grid=(nq,),
            in_specs=[
                pl.BlockSpec((nt, 2 * tr, width), lambda q, *_: (0, 0, 0)),
                pl.BlockSpec((1,) + piece, lambda q, *_: (q, 0, 0, 0)),
                pl.BlockSpec((tr, width), lambda q, *_: (0, 0)),
            ],
            out_specs=[
                pl.BlockSpec((tr, width), lambda q, *_: (0, 0)),
                pl.BlockSpec((width, pw), lambda q, *_: (0, q)),
                pl.BlockSpec((width, pw), lambda q, *_: (0, q)),
                pl.BlockSpec((pw, width), lambda q, *_: (q, 0)),
            ],
            scratch_shapes=[pltpu.VMEM((width, rows), bf16), pltpu.VMEM((rows, width), bf16)],
        ),
        out_shape=(
            jax.ShapeDtypeStruct((tr, width), bf16),
            jax.ShapeDtypeStruct((width, hidden_width), f32),
            jax.ShapeDtypeStruct((width, hidden_width), f32),
            jax.ShapeDtypeStruct((hidden_width, width), f32),
        ),
        compiler_params=pltpu.CompilerParams(vmem_limit_bytes=60 * 2**20),
        name="outer",
    )(gate_mask, up_mask, down_mask, gathered, act, d_tokens)
    return d_tokens, gate_sum, up_sum, down_sum


def solution(mesh):
    in_specs = (
        P("tensor", "dp"),
        P("tensor", "dp"),
        P("dp", "tensor"),
        P("dp", "tensor"),
        P("tensor", "dp"),
        P("dp", "tensor"),
        P("dp", "tensor"),
        P("tensor", "dp"),
        P("tensor"),
    )
    out_specs = (P("tensor", "dp"), P("dp", "tensor"), P("dp", "tensor"), P("tensor", "dp"))
    body = functools.partial(on_device, mesh.shape["dp"], mesh.shape["tensor"])
    return jax.shard_map(body, mesh=mesh, in_specs=in_specs, out_specs=out_specs, check_vma=False)
```

```python
import functools

import jax
import jax.numpy as jnp
from jax import lax
from jax.experimental import pallas as pl
from jax.experimental.pallas import tpu as pltpu
from jax.sharding import PartitionSpec as P

MESH = pl.DeviceIdType.MESH
LANES = 128
AHEAD = 6
bf16, f32 = jnp.bfloat16, jnp.float32


def dot_nn(a, b):
    return jnp.dot(a, b, preferred_element_type=f32)


def dot_nt(a, b):
    return lax.dot_general(a, b, (((1,), (1,)), ((), ())), preferred_element_type=f32)


def keep_tile(keeps):
    tiles = [jnp.full((16, LANES), k.astype(f32), f32).astype(bf16) for k in keeps]
    return jnp.concatenate(tiles, axis=1) if len(tiles) > 1 else tiles[0]


def masked(rows, keeps):
    count, cols = rows.shape
    return (rows.reshape(count // 16, 16, cols) * keep_tile(keeps)[None]).reshape(count, cols)


def masked_stack(rows, keep_lists):
    copies = [masked(rows, keeps) for keeps in keep_lists]
    return jnp.concatenate(copies, axis=0) if len(copies) > 1 else copies[0]


def swiglu_parts(gate_pre, up_pre, hidden_grad):
    sig = jax.nn.sigmoid(gate_pre)
    activated = gate_pre * sig
    hidden = (activated * up_pre).astype(bf16)
    gate_grad = (hidden_grad * up_pre * sig * (1.0 + gate_pre * (1.0 - sig))).astype(bf16)
    up_grad = (hidden_grad * activated).astype(bf16)
    return gate_grad, up_grad, hidden


def exchange_kernel(
    ndp, nt, nq, pw, nchunk,
    tok_ref, cot_ref, gate_hbm, up_hbm, down_hbm, gmask, umask, dmask, counts,
    dtok_ref, act_ref, x_ref,
    gw, uw, dw, xs, tokall, cotall, snd1, own1, rcv1, snd2, rcv2, acts, dacc, dsnd, drcv,
    wsem, out_sem, xs_s, xs_r, s1_s, s1_r, s2_s, s2_r, ag_s, ag_r, fw_s, fw_r, dt_s, dt_r,
):
    nchip = ndp // 2
    tr, width = tok_ref.shape
    kblocks = width // LANES
    me = lax.axis_index("dp")
    mt = lax.axis_index("tensor")
    core = lax.rem(me, 2)
    chip = me // 2
    sibling = chip * 2 + (1 - core)

    def weight_copies(q):
        cols = pl.ds(pl.multiple_of(q * pw, pw), pw)
        return (
            pltpu.make_async_copy(gate_hbm.at[:, cols], gw.at[q], wsem.at[q, 0]),
            pltpu.make_async_copy(up_hbm.at[:, cols], uw.at[q], wsem.at[q, 1]),
            pltpu.make_async_copy(down_hbm.at[cols, :], dw.at[q], wsem.at[q, 2]),
        )

    def each_piece(c, k, last):
        return c * ndp + 2 * k + (core if last else 1 - core)

    def load(i, _):
        within = lax.rem(i, ndp)
        q = (i // ndp) * ndp + (within // 2) * 2 + jnp.where(lax.rem(i, 2) == 0, 1 - core, core)

        @pl.when(jnp.logical_and(i < nchunk * ndp, q < nq))
        def _():
            for copy in weight_copies(q):
                copy.start()
        return 0

    lax.fori_loop(0, AHEAD, load, 0)

    live = lax.broadcasted_iota(jnp.int32, (tr, width), 0) < counts[0]
    cot = jnp.where(live, cot_ref[...].astype(f32), 0.0)
    xs[mt] = jnp.concatenate([tok_ref[...].astype(f32), cot], axis=0).astype(bf16)

    barrier = pltpu.get_barrier_semaphore()
    pl.semaphore_signal(barrier, inc=1, device_id=(sibling, mt), device_id_type=MESH)

    def greet_chip(j, _):
        peer = lax.rem(chip + j, nchip) * 2 + core
        pl.semaphore_signal(barrier, inc=1, device_id=(peer, mt), device_id_type=MESH)
        return 0

    def greet_tensor(j, _):
        pl.semaphore_signal(barrier, inc=1, device_id=(me, lax.rem(mt + j, nt)), device_id_type=MESH)
        return 0

    lax.fori_loop(1, nchip, greet_chip, 0)
    lax.fori_loop(1, nt, greet_tensor, 0)
    pl.semaphore_wait(barrier, 1 + (nchip - 1) + (nt - 1))

    def x_copy(slot, j, peer):
        return pltpu.make_async_remote_copy(
            src_ref=xs.at[slot], dst_ref=xs.at[slot], send_sem=xs_s.at[j],
            recv_sem=xs_r.at[slot], device_id=(me, peer), device_id_type=MESH)

    def x_send(j, _):
        x_copy(mt, j, lax.rem(mt + j, nt)).start()
        return 0

    def x_wait(j, _):
        peer = lax.rem(mt + j, nt)
        x_copy(peer, j, peer).wait_recv()
        return 0

    def x_sent(j, _):
        x_copy(mt, j, lax.rem(mt + j, nt)).wait_send()
        return 0

    lax.fori_loop(1, nt, x_send, 0)
    lax.fori_loop(1, nt, x_wait, 0)
    gathered = xs[...].astype(f32)
    tokall[...] = gathered[:, :tr].reshape(nt * tr, width).astype(bf16)
    cotall[...] = gathered[:, tr:].reshape(nt * tr, width).astype(bf16)
    x_out = pltpu.make_async_copy(xs, x_ref, out_sem.at[nchunk])
    x_out.start()
    rows = nt * tr
    per = pw // LANES
    pair = 2 if kblocks % 2 == 0 else 1

    def forward_piece(q, out):
        @pl.when(q < nq)
        def _():
            for copy in weight_copies(q):
                copy.wait()
            for w, mask, slot in ((gw, gmask, 0), (uw, umask, 1), (dw, dmask, 2)):
                source = cotall if slot == 2 else tokall
                left = masked_stack(
                    source[...],
                    [[mask[kb, q * per + i] for kb in range(kblocks)] for i in range(per)])
                sums = dot_nt(left, w[q]) if slot == 2 else dot_nn(left, w[q])
                for i in range(per):
                    cols = slice(i * LANES, (i + 1) * LANES)
                    out[slot, :, cols] = sums[i * rows:(i + 1) * rows, cols]

        @pl.when(q >= nq)
        def _():
            out[...] = jnp.zeros(out.shape, out.dtype)

    def copy1(c, k):
        return pltpu.make_async_remote_copy(
            src_ref=snd1.at[c, k], dst_ref=rcv1.at[c, k], send_sem=s1_s.at[c, k],
            recv_sem=s1_r.at[c, k], device_id=(sibling, mt), device_id_type=MESH)

    def forward(c, lo, hi):
        def step(k, _):
            load(c * ndp + 2 * k + AHEAD, 0)
            forward_piece(each_piece(c, k, False), snd1.at[c, k])
            copy1(c, k).start()
            load(c * ndp + 2 * k + 1 + AHEAD, 0)
            forward_piece(each_piece(c, k, True), own1.at[c, k])
            return 0
        lax.fori_loop(lo, hi, step, 0)

    def copy2(c, slot, k):
        return pltpu.make_async_remote_copy(
            src_ref=snd2.at[c, k], dst_ref=rcv2.at[c, slot], send_sem=s2_s.at[c, k],
            recv_sem=s2_r.at[c, slot], device_id=(k * 2 + core, mt), device_id_type=MESH)

    def reduce_send(c):
        def step(j, _):
            k = lax.rem(chip + j, nchip)
            copy1(c, k).wait_recv()
            snd2[c, k] = (own1[c, k] + rcv1[c, k]).astype(bf16)
            copy2(c, chip, k).start()
            return 0
        lax.fori_loop(1, nchip, step, 0)
        copy1(c, chip).wait_recv()

    def gather_copy(c, origin, sem, k):
        slot = c * ndp + origin
        return pltpu.make_async_remote_copy(
            src_ref=acts.at[slot], dst_ref=acts.at[slot], send_sem=ag_s.at[c, sem],
            recv_sem=ag_r.at[c, origin // 2], device_id=(k * 2 + core, mt), device_id_type=MESH)

    def sibling_copy(c, origin):
        slot = c * ndp + origin
        return pltpu.make_async_remote_copy(
            src_ref=acts.at[slot], dst_ref=acts.at[slot], send_sem=fw_s.at[c, origin // 2],
            recv_sem=fw_r.at[c, origin // 2], device_id=(sibling, mt), device_id_type=MESH)

    def activate(c):
        own1[c, chip] = own1[c, chip] + rcv1[c, chip]

        def add(j, _):
            k = lax.rem(chip + j, nchip)
            copy2(c, k, k).wait_recv()
            own1[c, chip] = own1[c, chip] + rcv2[c, k].astype(f32)
            return 0
        lax.fori_loop(1, nchip, add, 0)
        parts = swiglu_parts(own1[c, chip, 0], own1[c, chip, 1], own1[c, chip, 2])
        for i in range(3):
            acts[c * ndp + me, i] = parts[i]

        def send(j, _):
            gather_copy(c, me, j, lax.rem(chip + j, nchip)).start()
            return 0
        lax.fori_loop(1, nchip, send, 0)
        sibling_copy(c, me).start()

    def forward_on(c):
        def step(j, _):
            k = lax.rem(chip + j, nchip)
            gather_copy(c, k * 2 + core, j, k).wait_recv()
            sibling_copy(c, k * 2 + core).start()
            return 0
        lax.fori_loop(1, nchip, step, 0)

        def wait(k, _):
            sibling_copy(c, k * 2 + 1 - core).wait_recv()
            return 0
        lax.fori_loop(0, nchip, wait, 0)

    def token_grad(lo, hi):
        def step(q, _):
            for first in range(0, kblocks, pair):
                blocks = range(first, first + pair)
                span = pl.ds(first * LANES, pair * LANES)
                sums = None
                for w, mask, slot in ((gw, gmask, 0), (uw, umask, 1)):
                    left = masked_stack(
                        acts[q, slot], [[mask[kb, q * per + i] for i in range(per)] for kb in blocks])
                    term = dot_nt(left, w[q, span, :])
                    sums = term if sums is None else sums + term
                for i, kb in enumerate(blocks):
                    cols = slice(i * LANES, (i + 1) * LANES)
                    dacc[:, kb * LANES:(kb + 1) * LANES] += sums[i * rows:(i + 1) * rows, cols]
            return 0
        if hi > lo:
            lax.fori_loop(lo, hi, step, 0)

    def act_out(c):
        span = pl.ds(c * ndp, ndp)
        return pltpu.make_async_copy(acts.at[span], act_ref.at[span], out_sem.at[c])

    dacc[...] = jnp.zeros(dacc.shape, f32)
    for c in range(nchunk):
        forward(c, 0, nchip // 2)
        if c > 0:
            activate(c - 1)
        forward(c, nchip // 2, nchip)
        reduce_send(c)
        if c > 0:
            forward_on(c - 1)
            act_out(c - 1).start()
    done = min((nchunk - 1) * ndp, nq)
    token_grad(0, done // 2)
    activate(nchunk - 1)
    token_grad(done // 2, done)
    forward_on(nchunk - 1)
    act_out(nchunk - 1).start()
    token_grad(done, nq)

    dsnd[...] = dacc[...].reshape(nt, tr, width)

    def d_copy(slot, k):
        return pltpu.make_async_remote_copy(
            src_ref=dsnd.at[k], dst_ref=drcv.at[slot], send_sem=dt_s.at[k],
            recv_sem=dt_r.at[slot], device_id=(me, k), device_id_type=MESH)

    def d_send(j, _):
        k = lax.rem(mt + nt - j, nt)
        d_copy(mt, k).start()
        return 0

    lax.fori_loop(1, nt, d_send, 0)
    lax.fori_loop(1, nt, x_sent, 0)
    for c in range(nchunk):
        def drain(k, _, c=c):
            copy1(c, k).wait_send()
            sibling_copy(c, k * 2 + core).wait_send()
            return 0

        def drain_chips(j, _, c=c):
            k = lax.rem(chip + j, nchip)
            copy2(c, chip, k).wait_send()
            gather_copy(c, me, j, k).wait_send()
            return 0
        lax.fori_loop(0, nchip, drain, 0)
        lax.fori_loop(1, nchip, drain_chips, 0)

    def d_add(j, total):
        k = lax.rem(mt + j, nt)
        d_copy(k, k).wait_recv()
        return total + drcv[k]

    dtok_ref[...] = lax.fori_loop(1, nt, d_add, dsnd[mt]).astype(bf16)

    def d_sent(j, _):
        d_copy(mt, lax.rem(mt + j, nt)).wait_send()
        return 0
    lax.fori_loop(1, nt, d_sent, 0)
    x_out.wait()
    for c in range(nchunk):
        act_out(c).wait()


def outer_kernel(
    pw, gmask, umask, dmask, x_ref, act_ref, dtok_ref, dtok_out, gsum_ref, usum_ref, dsum_ref, tok_t, cot
):
    q = pl.program_id(0)
    nt, pair_rows, width = x_ref.shape
    tr = pair_rows // 2
    per = pw // LANES

    @pl.when(q == 0)
    def _():
        gathered = x_ref[...].astype(f32)
        tok_t[...] = gathered[:, :tr].reshape(nt * tr, width).T.astype(bf16)
        cot[...] = gathered[:, tr:].reshape(nt * tr, width).astype(bf16)
        dtok_out[...] = dtok_ref[...]

    for slot, mask, out in ((0, gmask, gsum_ref), (1, umask, usum_ref)):
        for kb in range(width // LANES):
            span = pl.ds(kb * LANES, LANES)
            block = dot_nn(tok_t[span, :], act_ref[0, slot])
            for i in range(per):
                cols = slice(i * LANES, (i + 1) * LANES)
                out[span, cols] = block[:, cols] * mask[kb, q * per + i].astype(f32)
    hidden_t = act_ref[0, 2].astype(f32).T.astype(bf16)
    for i in range(per):
        block = dot_nn(hidden_t[i * LANES:(i + 1) * LANES], cot[...])
        for kb in range(width // LANES):
            cols = slice(kb * LANES, (kb + 1) * LANES)
            dsum_ref[pl.ds(i * LANES, LANES), cols] = block[:, cols] * dmask[kb, q * per + i].astype(f32)


def on_device(
    ndp, nt, tokens, out_grad, gate_weight, up_weight, down_weight, gate_mask, up_mask, down_mask, counts
):
    tr, width = tokens.shape
    hidden_width = gate_weight.shape[1]
    rows = nt * tr
    pw = 2 * LANES if hidden_width % (2 * LANES) == 0 else LANES
    nq = hidden_width // pw
    nchunk = -(-nq // ndp)
    nchip = ndp // 2
    vmem = pl.BlockSpec(memory_space=pltpu.VMEM)
    smem = pl.BlockSpec(memory_space=pltpu.SMEM)
    hbm = pl.BlockSpec(memory_space=pl.ANY)
    dma = pltpu.SemaphoreType.DMA
    piece = (3, rows, pw)
    down_mask = down_mask.T
    d_tokens, act, gathered = pl.pallas_call(
        functools.partial(exchange_kernel, ndp, nt, nq, pw, nchunk),
        out_shape=(
            jax.ShapeDtypeStruct((tr, width), bf16),
            jax.ShapeDtypeStruct((nchunk * ndp,) + piece, bf16),
            jax.ShapeDtypeStruct((nt, 2 * tr, width), bf16),
        ),
        in_specs=[vmem, vmem, hbm, hbm, hbm, smem, smem, smem, smem],
        out_specs=(vmem, hbm, hbm),
        scratch_shapes=[
            pltpu.VMEM((nq, width, pw), bf16),
            pltpu.VMEM((nq, width, pw), bf16),
            pltpu.VMEM((nq, pw, width), bf16),
            pltpu.VMEM((nt, 2 * tr, width), bf16),
            pltpu.VMEM((rows, width), bf16),
            pltpu.VMEM((rows, width), bf16),
            pltpu.VMEM((nchunk, nchip) + piece, f32),
            pltpu.VMEM((nchunk, nchip) + piece, f32),
            pltpu.VMEM((nchunk, nchip) + piece, f32),
            pltpu.VMEM((nchunk, nchip) + piece, bf16),
            pltpu.VMEM((nchunk, nchip) + piece, bf16),
            pltpu.VMEM((nchunk * ndp,) + piece, bf16),
            pltpu.VMEM((rows, width), f32),
            pltpu.VMEM((nt, tr, width), f32),
            pltpu.VMEM((nt, tr, width), f32),
            dma((nq, 3)), dma((nchunk + 1,)),
            dma((nt,)), dma((nt,)),
            dma((nchunk, nchip)), dma((nchunk, nchip)),
            dma((nchunk, nchip)), dma((nchunk, nchip)),
            dma((nchunk, nchip)), dma((nchunk, nchip)),
            dma((nchunk, nchip)), dma((nchunk, nchip)),
            dma((nt,)), dma((nt,)),
        ],
        compiler_params=pltpu.CompilerParams(
            collective_id=0, has_side_effects=True, vmem_limit_bytes=58 * 2**20
        ),
        name="exchange",
    )(tokens, out_grad, gate_weight, up_weight, down_weight, gate_mask, up_mask, down_mask, counts)

    d_tokens, gate_sum, up_sum, down_sum = pl.pallas_call(
        functools.partial(outer_kernel, pw),
        grid_spec=pltpu.PrefetchScalarGridSpec(
            num_scalar_prefetch=3,
            grid=(nq,),
            in_specs=[
                pl.BlockSpec((nt, 2 * tr, width), lambda q, *_: (0, 0, 0)),
                pl.BlockSpec((1,) + piece, lambda q, *_: (q, 0, 0, 0)),
                pl.BlockSpec((tr, width), lambda q, *_: (0, 0)),
            ],
            out_specs=[
                pl.BlockSpec((tr, width), lambda q, *_: (0, 0)),
                pl.BlockSpec((width, pw), lambda q, *_: (0, q)),
                pl.BlockSpec((width, pw), lambda q, *_: (0, q)),
                pl.BlockSpec((pw, width), lambda q, *_: (q, 0)),
            ],
            scratch_shapes=[pltpu.VMEM((width, rows), bf16), pltpu.VMEM((rows, width), bf16)],
        ),
        out_shape=(
            jax.ShapeDtypeStruct((tr, width), bf16),
            jax.ShapeDtypeStruct((width, hidden_width), f32),
            jax.ShapeDtypeStruct((width, hidden_width), f32),
            jax.ShapeDtypeStruct((hidden_width, width), f32),
        ),
        compiler_params=pltpu.CompilerParams(vmem_limit_bytes=60 * 2**20),
        name="outer",
    )(gate_mask, up_mask, down_mask, gathered, act, d_tokens)
    return d_tokens, gate_sum, up_sum, down_sum


def solution(mesh):
    in_specs = (
        P("tensor", "dp"),
        P("tensor", "dp"),
        P("dp", "tensor"),
        P("dp", "tensor"),
        P("tensor", "dp"),
        P("dp", "tensor"),
        P("dp", "tensor"),
        P("tensor", "dp"),
        P("tensor"),
    )
    out_specs = (P("tensor", "dp"), P("dp", "tensor"), P("dp", "tensor"), P("tensor", "dp"))
    body = functools.partial(on_device, mesh.shape["dp"], mesh.shape["tensor"])
    return jax.shard_map(body, mesh=mesh, in_specs=in_specs, out_specs=out_specs, check_vma=False)
```
